32 devices in a mesh: frames: 16 (over z, y, x), rows: 2 (over core).
Axes of the slice: x: 2, y: 2, z: 4, core: 2. Of those that a mesh axis runs over, the one named last changes fastest.
Arguments:
- video: bfloat16 [128, 8, 16, 384], P('frames', 'rows'), may hold values from -6 to 6
- counts: int32 [16], replicated, may hold values from 1 to 8, as said below
- down_weight: bfloat16 [9, 384, 384], replicated, may hold values from -0.109375 to 0.109375
- spatial_conv_bias: float32 [384], replicated, may hold values from -1.5 to 1.5
- time_weight: bfloat16 [3, 384, 384], replicated, may hold values from -0.1875 to 0.1875
- time_bias: float32 [384], replicated, may hold values from -1.5 to 1.5
- norm1_gain: float32 [384], replicated, may hold values from 0.1 to 1.9
- conv1_weight: bfloat16 [27, 384, 384], P(None, 'rows'), may hold values from -0.0625 to 0.0625
- conv1_bias: float32 [384], P('rows'), may hold values from -1.5 to 1.5
- norm2_gain: float32 [384], replicated, may hold values from 0.1 to 1.9
- conv2_weight: bfloat16 [27, 384, 384], P(None, 'rows'), may hold values from -0.0625 to 0.0625
- conv2_bias: float32 [384], P('rows'), may hold values from -1.5 to 1.5
Outputs:
- latents: bfloat16 [64, 4, 8, 384], P('frames', 'rows')
The draws below stay inside these ranges and needn't reach their ends.
Inputs may be any that keep to these rules, and one draw needn't show every extreme that they name: `counts`: entry 0 is 1; every other entry is even and at least 4; some entry equals 8.
All inputs are finite; a program needn't handle non-finite values.
Results may differ from the reference program's by a relative error of at most 0.0065.
Values may be sent and summed in bfloat16 or wider, within the bound.
A program may use at most 64 MiB of HBM per device.

```python
import jax
import jax.numpy as jnp
from jax import lax

CHANNEL_COUNT = 384
FCAP = 8
INPUT_COLUMNS = 16
OCAP = 4
OUTPUT_COLUMNS = 8
SLOT_TOTAL = 128
NOUT = 64
INPUT_ROWS = 8
OUTPUT_ROWS = 4
N_FRAMES = 16


def draw_counts(key, part):
    key = jax.random.fold_in(key, 11)
    key_half, key_full = jax.random.split(key)
    halves = jax.random.randint(key_half, (N_FRAMES,), 2, FCAP // 2 + 1)
    fullest = jax.random.randint(key_full, (), 1, N_FRAMES)
    index_all = jnp.arange(N_FRAMES, dtype=jnp.int32)
    sizes_all = jnp.where(index_all == fullest, FCAP, 2 * halves)
    return jnp.where(index_all == 0, 1, sizes_all).astype(jnp.int32)


def shard_levels(rng, shape, shards, smallest, largest):
    def one(axis_at, blocks):
        steps = jax.random.uniform(jax.random.fold_in(jax.random.fold_in(rng, 6), axis_at), (blocks,), jnp.float32, smallest / len(shards), largest / len(shards))
        return jnp.repeat(jnp.exp(steps), shape[axis_at] // blocks).reshape((-1,) + (1,) * (len(shape) - axis_at - 1))

    level = one(*shards[0])
    for cut in shards[1:]:
        level = level * one(*cut)
    return level


def gaussian(key, shape, scale, reach, pieces=(), held_as=jnp.bfloat16):
    array = jax.random.normal(key, shape, jnp.float32) * scale
    if len(pieces) > 0:
        array = shard_levels(key, shape, pieces, -0.22, 0.18) * array
    return jnp.clip(array, min=-reach, max=reach).astype(held_as)


def setup_inputs(seed: int = 0) -> dict:
    splits = jax.random.split(jax.random.key(seed), 13)
    return {
        "video": gaussian(splits[0], (SLOT_TOTAL, INPUT_ROWS, INPUT_COLUMNS, CHANNEL_COUNT), 1.0, 6.0, ((0, 16), (1, 2))),
        "counts": draw_counts(jax.random.fold_in(splits[12], 71), 0),
        "down_weight": gaussian(splits[2], (9, CHANNEL_COUNT, CHANNEL_COUNT), (9 * CHANNEL_COUNT) ** -0.5, 0.109375),
        "spatial_conv_bias": gaussian(splits[3], (CHANNEL_COUNT,), 0.3, 1.5, (), jnp.float32),
        "time_weight": gaussian(splits[4], (3, CHANNEL_COUNT, CHANNEL_COUNT), (3 * CHANNEL_COUNT) ** -0.5, 0.1875),
        "time_bias": gaussian(splits[5], (CHANNEL_COUNT,), 0.3, 1.5, (), jnp.float32),
        "norm1_gain": jnp.clip(1.0 + 0.18 * jax.random.normal(splits[6], (CHANNEL_COUNT,), jnp.float32), 0.1, 1.9),
        "conv1_weight": gaussian(splits[7], (27, CHANNEL_COUNT, CHANNEL_COUNT), (27 * CHANNEL_COUNT) ** -0.5, 0.0625, ((1, 2),)),
        "conv1_bias": gaussian(splits[8], (CHANNEL_COUNT,), 0.3, 1.5, ((0, 2),), jnp.float32),
        "norm2_gain": jnp.clip(1.0 + 0.18 * jax.random.normal(splits[9], (CHANNEL_COUNT,), jnp.float32), 0.1, 1.9),
        "conv2_weight": gaussian(splits[10], (27, CHANNEL_COUNT, CHANNEL_COUNT), (27 * CHANNEL_COUNT) ** -0.5, 0.0625, ((1, 2),)),
        "conv2_bias": gaussian(splits[11], (CHANNEL_COUNT,), 0.3, 1.5, ((0, 2),), jnp.float32),
    }


epsilon = 1e-06

def rms_scale(values, gain_vec):
    mean_sq = lax.optimization_barrier(jnp.mean(values * values, axis=-1, keepdims=True))
    return values * lax.rsqrt(mean_sq + epsilon) * gain_vec

def conv_taps(padded, weight, frames_out, rows_out, cols_out):
    running = None
    for tap_t in range(3):
        for tap_r in range(3):
            for tap_c in range(3):
                window = padded[tap_t:tap_t + frames_out, tap_r:tap_r + rows_out, tap_c:tap_c + cols_out]
                flat_rows = window.reshape(-1, window.shape[-1])
                partial_term = lax.dot_general(flat_rows, weight[tap_t * 9 + tap_r * 3 + tap_c], (((1,), (1,)), ((), ())), preferred_element_type=jnp.float32)
                running = partial_term if running is None else running + partial_term
    return running.reshape(frames_out, rows_out, cols_out, weight.shape[1])

def causal_pad(values):
    return jnp.pad(values, ((2, 0), (1, 1), (1, 1), (0, 0)))

def reference(video, counts, down_weight, spatial_conv_bias, time_weight, time_bias, norm1_gain, conv1_weight, conv1_bias, norm2_gain, conv2_weight, conv2_bias):
    extended = jnp.pad(video, ((0, 0), (0, 1), (0, 1), (0, 0)))
    spatial_result = None
    for tap_r in range(3):
        for tap_c in range(3):
            window = extended[:, tap_r:tap_r + 2 * OUTPUT_ROWS:2, tap_c:tap_c + 2 * OUTPUT_COLUMNS:2]
            partial_term = jnp.dot(window.reshape(-1, CHANNEL_COUNT), down_weight[tap_r * 3 + tap_c], preferred_element_type=jnp.float32)
            spatial_result = partial_term if spatial_result is None else spatial_result + partial_term
    halved_frames = (spatial_result + spatial_conv_bias).astype(jnp.bfloat16).reshape(SLOT_TOTAL, OUTPUT_ROWS, OUTPUT_COLUMNS, CHANNEL_COUNT)
    slot_numbers = jnp.arange(SLOT_TOTAL, dtype=jnp.int32)
    owning_shard = slot_numbers // FCAP
    local_position = slot_numbers % FCAP
    shard_starts = (jnp.cumsum(counts) - counts).astype(jnp.int32)
    valid_mask = local_position < counts[owning_shard]
    frame_placement = jnp.where(valid_mask, shard_starts[owning_shard] + local_position, SLOT_TOTAL).astype(jnp.int32)
    slot_lookup = jnp.zeros((SLOT_TOTAL + 1,), jnp.int32).at[frame_placement].set(slot_numbers)
    packed_frames = halved_frames[slot_lookup[:SLOT_TOTAL]]
    merged = None
    for tap_t in range(3):
        window = packed_frames[tap_t:tap_t + 2 * (NOUT - 1):2]
        partial_term = jnp.dot(window.reshape(-1, CHANNEL_COUNT), time_weight[tap_t], preferred_element_type=jnp.float32)
        merged = partial_term if merged is None else merged + partial_term
    merged = (merged + time_bias).reshape(NOUT - 1, OUTPUT_ROWS, OUTPUT_COLUMNS, CHANNEL_COUNT)
    latent_in = jnp.concatenate([packed_frames[0:1].astype(jnp.float32), merged], axis=0).astype(jnp.bfloat16)
    act_one = jax.nn.silu(rms_scale(latent_in.astype(jnp.float32), norm1_gain)).astype(jnp.bfloat16)
    h_one = (conv_taps(causal_pad(act_one), conv1_weight, NOUT, OUTPUT_ROWS, OUTPUT_COLUMNS) + conv1_bias).astype(jnp.bfloat16)
    act_two = jax.nn.silu(rms_scale(h_one.astype(jnp.float32), norm2_gain)).astype(jnp.bfloat16)
    h_two = (conv_taps(causal_pad(act_two), conv2_weight, NOUT, OUTPUT_ROWS, OUTPUT_COLUMNS) + conv2_bias).astype(jnp.bfloat16)
    joined = (latent_in.astype(jnp.float32) + h_two.astype(jnp.float32)).astype(jnp.bfloat16)
    out_ids = jnp.arange(NOUT, dtype=jnp.int32)
    out_owner = out_ids // OCAP
    out_within = out_ids % OCAP
    live_counts = jnp.where(out_owner == 0, 1, counts[out_owner] // 2)
    target = jnp.where(out_owner == 0, 0, (shard_starts[out_owner] + 1) // 2 + out_within)
    used = out_within < live_counts
    target = jnp.where(used, target, 0).astype(jnp.int32)
    picked = joined[target]
    return jnp.where(used[:, None, None, None], picked, jnp.zeros_like(picked))
```

```python
import functools

import jax
import jax.numpy as jnp
from jax import lax
from jax.experimental import pallas as pl
from jax.experimental.pallas import tpu as pltpu
from jax.sharding import PartitionSpec as P

MESH = pl.DeviceIdType.MESH
F32 = jnp.float32
BF16 = jnp.bfloat16
EPSILON = 1e-06
LANES = 128
LEFT = 8


def rms_silu(values, gain):
    mean_sq = jnp.mean(values * values, axis=-1, keepdims=True)
    return jax.nn.silu(values * lax.rsqrt(mean_sq + EPSILON) * gain)


def round16(values):
    return values.astype(BF16).astype(F32)


def join(row, own, other):
    low = jnp.where(row == 0, own, other)
    high = jnp.where(row == 0, other, own)
    return jnp.concatenate([low, high], axis=-1)


def dot_t(values, weight):
    return lax.dot_general(values, weight, (((1,), (1,)), ((), ())), preferred_element_type=F32)


def kernel(
    shards,
    video,
    counts,
    down_weight,
    spatial_bias,
    time_weight,
    time_bias,
    gain1,
    weight1,
    bias1,
    gain2,
    weight2,
    bias2,
    out,
    vid_v,
    halo_v,
    down_v,
    time_v,
    w1_v,
    w2_v,
    xf,
    xs,
    timeline,
    red_own,
    red_other,
    last_red,
    before_v,
    lat_v,
    padded,
    patches,
    last_act,
    prior_act,
    hid,
    h_own,
    h_other,
    h_last,
    h_prior,
    h2_send,
    h2_recv,
    in_sem,
    down_sem,
    w1_sem,
    w2_sem,
    send_sem,
    recv_sem,
    before_sem,
    prior_sem,
):
    shard = lax.axis_index("frames")
    row = lax.axis_index("rows")
    other = 1 - row
    slots, in_rows, in_cols, chans = vid_v.shape
    out_slots, own_rows, cols = slots // 2, in_rows // 2, in_cols // 2
    all_rows = 2 * own_rows
    half = h_own.shape[1]
    plane = all_rows * cols
    has_next = shard < shards - 1
    has_prev = shard > 0

    vid_copy = pltpu.make_async_copy(video, vid_v, in_sem.at[0])
    vid_copy.start()
    down_copies = []
    for k in range(3):
        copy = pltpu.make_async_copy(
            down_weight.at[pl.ds(3 * k, 3)], down_v.at[pl.ds(3 * k, 3)], down_sem.at[k]
        )
        copy.start()
        down_copies.append(copy)

    barrier = pltpu.get_barrier_semaphore()
    pl.semaphore_signal(barrier, inc=1, device_id=(shard, other), device_id_type=MESH)

    @pl.when(has_next)
    def _():
        for r in range(2):
            pl.semaphore_signal(barrier, inc=1, device_id=(shard + 1, r), device_id_type=MESH)

    @pl.when(has_prev)
    def _():
        for r in range(2):
            pl.semaphore_signal(barrier, inc=1, device_id=(shard - 1, r), device_id_type=MESH)

    time_copy = pltpu.make_async_copy(time_weight, time_v, in_sem.at[1])
    time_copy.start()

    def start_weight(source, target, sems):
        copies = {}
        for kt in (2, 1, 0):
            for tap in range(9 * kt, 9 * kt + 9):
                copies[tap] = pltpu.make_async_copy(
                    source.at[tap], target.at[:, pl.ds(tap * chans, chans)], sems.at[tap]
                )
                copies[tap].start()
        return copies

    w1_copies = start_weight(weight1, w1_v, w1_sem)
    w2_copies = start_weight(weight2, w2_v, w2_sem)

    own_count = counts[shard]
    live = jnp.where(shard == 0, 1, own_count // 2)

    pl.semaphore_wait(
        barrier, 1 + jnp.where(has_next, 2, 0) + jnp.where(has_prev, 2, 0)
    )

    def remote(source, target, index, device, recv=None):
        return pltpu.make_async_remote_copy(
            src_ref=source,
            dst_ref=target,
            send_sem=send_sem.at[index],
            recv_sem=recv_sem.at[index] if recv is None else recv,
            device_id=device,
            device_id_type=MESH,
        )

    halo_copy = remote(video.at[:, 0], halo_v, 0, (shard, other))

    @pl.when(row == 1)
    def _():
        halo_copy.start()
        halo_v[...] = jnp.zeros_like(halo_v)

    padded[...] = jnp.zeros_like(padded)
    hid[0:2] = jnp.zeros((2,) + hid.shape[1:], F32)
    xf[:, :, :, in_cols:] = jnp.zeros(xf.shape[:3] + (xf.shape[3] - in_cols, LANES), F32)

    def spread(line, values):
        values = values.astype(F32)
        for lanes in range(chans // LANES):
            begin = lanes * LANES
            xf[line, lanes, :, 0:in_cols] = values[:, :, begin : begin + LANES]
            for tc in range(3):
                part = xf[line, lanes, :, pl.ds(tc, cols, stride=2), :]
                at = tc * chans + begin
                xs[line, :, at : at + LANES] = part.reshape(slots * cols, LANES).astype(BF16)

    vid_copy.wait()
    for line in range(in_rows):
        spread(line, vid_v[:, line])

    total = None
    for tr in range(3):
        if tr == 2:

            @pl.when(row == 0)
            def _():
                halo_copy.wait_recv()

            spread(in_rows, halo_v[...])
        down_copies[tr].wait()
        lines = jnp.concatenate([xs[2 * r + tr] for r in range(own_rows)], axis=0)
        taps = down_v[3 * tr : 3 * tr + 3].reshape(3 * chans, chans)
        part = jnp.dot(lines, taps, preferred_element_type=F32)
        total = part if total is None else total + part
    reduced = (total + spatial_bias[...]).astype(BF16)
    red_own[...] = reduced
    red_copy = remote(red_own, red_other, 1, (shard, other))
    red_copy.start()

    def to_timeline(values, first_row):
        values = values.astype(F32).reshape(own_rows, slots, cols, chans)
        for f in range(slots):
            timeline[f + 1, pl.ds(first_row, own_rows)] = values[:, f]

    to_timeline(reduced, own_rows * row)
    last_red[...] = (
        timeline[own_count, pl.ds(own_rows * row, own_rows)].reshape(own_rows * cols, chans).astype(BF16)
    )
    before_copies = [
        remote(last_red, before_v.at[row], 2 + r, (shard + 1, r), before_sem.at[row]) for r in range(2)
    ]

    def next_start(copies):
        @pl.when(has_next)
        def _():
            for copy in copies:
                copy.start()

    def prev_wait(copies, buffer):
        @pl.when(has_prev)
        def _():
            for copy in copies:
                copy.wait_recv()

        @pl.when(jnp.logical_not(has_prev))
        def _():
            buffer[...] = jnp.zeros_like(buffer)

    next_start(before_copies)
    before_waits = [
        remote(last_red, before_v.at[r], 2, (shard, other), before_sem.at[r]) for r in range(2)
    ]

    red_copy.wait_recv()
    to_timeline(red_other[...], own_rows * other)
    time_copy.wait()

    def tap_frames(kt):
        frames = [timeline[2 * t + kt].reshape(plane, chans) for t in range(out_slots)]
        return jnp.concatenate(frames, axis=0).astype(BF16)

    merged = None
    for kt in (2, 1, 0):
        if kt == 0:
            prev_wait(before_waits, before_v)
            timeline[0] = before_v[...].astype(F32).reshape(all_rows, cols, chans)
        part = jnp.dot(tap_frames(kt), time_v[kt], preferred_element_type=F32)
        merged = part if merged is None else merged + part
    merged = merged + time_bias[...]
    first = jnp.where(shard == 0, timeline[1].reshape(plane, chans), merged[:plane])
    latent = round16(jnp.concatenate([first, merged[plane:]], axis=0))
    lat_v[...] = latent.reshape(lat_v.shape)

    def place(first_frame, frames, values):
        padded[first_frame : first_frame + frames, 1 : 1 + all_rows, LEFT : LEFT + cols, :] = values.reshape(
            frames, all_rows, cols, chans
        )
        for kj in range(3):
            begin = LEFT - 1 + kj
            window = padded[first_frame : first_frame + frames, :, begin : begin + cols, :]
            for ki in range(3):
                tap = 3 * ki + kj
                patches[first_frame : first_frame + frames, :, tap * chans : (tap + 1) * chans] = (
                    window[:, ki : ki + all_rows].reshape(frames, plane, chans).astype(BF16)
                )

    def conv_part(kt, target, copies):
        for tap in range(9 * kt, 9 * kt + 9):
            copies[tap].wait()
        lines = patches[kt : kt + out_slots].reshape(out_slots * plane, 9 * chans)
        return dot_t(lines, target[:, 9 * kt * chans : 9 * (kt + 1) * chans])

    act_one = round16(rms_silu(latent, gain1[...]))
    place(2, out_slots, act_one)
    recent = padded[pl.ds(live, 2), 1 : 1 + all_rows, LEFT : LEFT + cols, :]
    last_act[...] = recent.reshape(2 * plane, chans).astype(BF16)
    act_copy = remote(last_act, prior_act, 4, (shard + 1, row))
    next_start([act_copy])
    acc = conv_part(2, w1_v, w1_copies)
    prev_wait([act_copy], prior_act)
    place(0, 2, prior_act[...].astype(F32))
    for kt in (1, 0):
        acc = acc + conv_part(kt, w1_v, w1_copies)
    part_one = (acc + bias1[...]).astype(BF16)
    h_own[...] = part_one
    h_copy = remote(h_own, h_other, 5, (shard, other))
    h_copy.start()
    hid[2 : 2 + out_slots] = part_one.astype(F32).reshape(out_slots, plane, half)
    h_last[...] = hid[pl.ds(live, 2)].reshape(2 * plane, half).astype(BF16)
    prior_copies = [
        remote(h_last, h_prior.at[row], 6 + r, (shard + 1, r), prior_sem.at[row]) for r in range(2)
    ]
    next_start(prior_copies)
    prior_waits = [
        remote(h_last, h_prior.at[r], 6, (shard, other), prior_sem.at[r]) for r in range(2)
    ]

    h_copy.wait_recv()
    hidden = join(row, part_one.astype(F32), h_other[...].astype(F32))
    place(2, out_slots, rms_silu(hidden, gain2[...]))
    acc = conv_part(2, w2_v, w2_copies)
    prev_wait(prior_waits, h_prior)
    hidden = jnp.concatenate([h_prior[0].astype(F32), h_prior[1].astype(F32)], axis=-1)
    place(0, 2, rms_silu(hidden, gain2[...]))
    for kt in (1, 0):
        acc = acc + conv_part(kt, w2_v, w2_copies)
    part_two = round16(acc + bias2[...]).reshape(out_slots, plane, half)
    hid[2 : 2 + out_slots] = part_two
    rows_of = own_rows * cols

    def share(which):
        return hid[2 : 2 + out_slots, pl.ds(which * rows_of, rows_of)].reshape(out_slots * rows_of, half)

    h2_send[...] = share(other).astype(BF16)
    h2_copy = remote(h2_send, h2_recv, 8, (shard, other))
    h2_copy.start()
    mine = share(row)
    kept = lat_v[:, pl.ds(own_rows * row, own_rows)]

    @pl.when(has_next)
    def _():
        for copy in before_copies + [act_copy] + prior_copies:
            copy.wait_send()

    @pl.when(row == 1)
    def _():
        halo_copy.wait_send()

    red_copy.wait_send()
    h_copy.wait_send()
    h2_copy.wait_recv()
    hidden = join(row, mine, h2_recv[...].astype(F32)).reshape(out_slots, own_rows, cols, chans)
    slot = lax.broadcasted_iota(jnp.int32, hidden.shape, 0)
    out[...] = jnp.where(slot < live, kept + hidden, 0.0).astype(out.dtype)
    h2_copy.wait_send()


def per_device(shards, video, counts, down, sbias, time, tbias, gain1, w1, b1, gain2, w2, b2):
    slots, in_rows, in_cols, chans = video.shape
    out_slots, own_rows, cols = slots // 2, in_rows // 2, in_cols // 2
    all_rows = 2 * own_rows
    half = w1.shape[1]
    plane = all_rows * cols
    hbm = pl.BlockSpec(memory_space=pl.ANY)
    vmem = pl.BlockSpec(memory_space=pltpu.VMEM)
    smem = pl.BlockSpec(memory_space=pltpu.SMEM)
    dma = pltpu.SemaphoreType.DMA
    return pl.pallas_call(
        functools.partial(kernel, shards),
        out_shape=jax.ShapeDtypeStruct((out_slots, own_rows, cols, chans), BF16),
        in_specs=[hbm, smem, hbm, vmem, hbm, vmem, vmem, hbm, vmem, vmem, hbm, vmem],
        out_specs=vmem,
        scratch_shapes=[
            pltpu.VMEM(video.shape, BF16),
            pltpu.VMEM((slots, in_cols, chans), BF16),
            pltpu.VMEM(down.shape, BF16),
            pltpu.VMEM(time.shape, BF16),
            pltpu.VMEM((half, 27 * chans), BF16),
            pltpu.VMEM((half, 27 * chans), BF16),
            pltpu.VMEM((in_rows + 1, chans // LANES, slots, in_cols + 8, LANES), F32),
            pltpu.VMEM((in_rows + 1, slots * cols, 3 * chans), BF16),
            pltpu.VMEM((slots + 1, all_rows, cols, chans), F32),
            pltpu.VMEM((own_rows * slots * cols, chans), BF16),
            pltpu.VMEM((own_rows * slots * cols, chans), BF16),
            pltpu.VMEM((own_rows * cols, chans), BF16),
            pltpu.VMEM((2, own_rows * cols, chans), BF16),
            pltpu.VMEM((out_slots, all_rows, cols, chans), F32),
            pltpu.VMEM((2 + out_slots, all_rows + 2, cols + 16, chans), F32),
            pltpu.VMEM((2 + out_slots, plane, 9 * chans), BF16),
            pltpu.VMEM((2 * plane, chans), BF16),
            pltpu.VMEM((2 * plane, chans), BF16),
            pltpu.VMEM((2 + out_slots, plane, half), F32),
            pltpu.VMEM((out_slots * plane, half), BF16),
            pltpu.VMEM((out_slots * plane, half), BF16),
            pltpu.VMEM((2 * plane, half), BF16),
            pltpu.VMEM((2, 2 * plane, half), BF16),
            pltpu.VMEM((out_slots * own_rows * cols, half), BF16),
            pltpu.VMEM((out_slots * own_rows * cols, half), BF16),
            dma((2,)),
            dma((3,)),
            dma((27,)),
            dma((27,)),
            dma((9,)),
            dma((9,)),
            dma((2,)),
            dma((2,)),
        ],
        compiler_params=pltpu.CompilerParams(
            collective_id=0, has_side_effects=True, vmem_limit_bytes=48 * 1024 * 1024
        ),
        name="section",
    )(
        video,
        counts,
        down,
        sbias.reshape(1, -1),
        time,
        tbias.reshape(1, -1),
        gain1.reshape(1, -1),
        w1,
        b1.reshape(1, -1),
        gain2.reshape(1, -1),
        w2,
        b2.reshape(1, -1),
    )


def solution(mesh):
    in_specs = (
        P("frames", "rows", None, None),
        P(),
        P(),
        P(),
        P(),
        P(),
        P(),
        P(None, "rows", None),
        P("rows"),
        P(),
        P(None, "rows", None),
        P("rows"),
    )
    return jax.shard_map(
        functools.partial(per_device, mesh.shape["frames"]),
        mesh=mesh,
        in_specs=in_specs,
        out_specs=P("frames", "rows", None, None),
        check_vma=False,
    )
```

```python
import functools

import jax
import jax.numpy as jnp
from jax import lax
from jax.experimental import pallas as pl
from jax.experimental.pallas import tpu as pltpu
from jax.sharding import PartitionSpec as P

MESH = pl.DeviceIdType.MESH
F32 = jnp.float32
BF16 = jnp.bfloat16
EPSILON = 1e-06
LANES = 128
LEFT = 8


def rms_silu(values, gain):
    mean_sq = jnp.mean(values * values, axis=-1, keepdims=True)
    return jax.nn.silu(values * lax.rsqrt(mean_sq + EPSILON) * gain)


def round16(values):
    return values.astype(BF16).astype(F32)


def join(row, own, other):
    low = jnp.where(row == 0, own, other)
    high = jnp.where(row == 0, other, own)
    return jnp.concatenate([low, high], axis=-1)


def dot_t(values, weight):
    return lax.dot_general(values, weight, (((1,), (1,)), ((), ())), preferred_element_type=F32)


def kernel(
    shards,
    video,
    counts_hbm,
    down_weight,
    spatial_bias_hbm,
    time_weight,
    time_bias_hbm,
    gain1_hbm,
    weight1,
    bias1_hbm,
    gain2_hbm,
    weight2,
    bias2_hbm,
    out,
    vid_v,
    halo_v,
    down_v,
    time_v,
    w1_v,
    w2_v,
    xf,
    xs,
    timeline,
    red_own,
    red_other,
    last_red,
    before_v,
    lat_v,
    padded,
    patches,
    last_act,
    prior_act,
    hid,
    h_own,
    h_other,
    h_last,
    h_prior,
    h2_send,
    h2_recv,
    in_sem,
    down_sem,
    w1_sem,
    w2_sem,
    send_sem,
    recv_sem,
    before_sem,
    prior_sem,
    counts,
    spatial_bias,
    time_bias,
    gain1,
    bias1,
    gain2,
    bias2,
    small_sem,
):
    shard = lax.axis_index("frames")
    row = lax.axis_index("rows")
    other = 1 - row
    slots, in_rows, in_cols, chans = vid_v.shape
    out_slots, own_rows, cols = slots // 2, in_rows // 2, in_cols // 2
    all_rows = 2 * own_rows
    half = h_own.shape[1]
    plane = all_rows * cols
    has_next = shard < shards - 1
    has_prev = shard > 0

    vid_copy = pltpu.make_async_copy(video, vid_v, in_sem.at[0])
    vid_copy.start()
    down_copies = []
    for k in range(3):
        copy = pltpu.make_async_copy(
            down_weight.at[pl.ds(3 * k, 3)], down_v.at[pl.ds(3 * k, 3)], down_sem.at[k]
        )
        copy.start()
        down_copies.append(copy)

    barrier = pltpu.get_barrier_semaphore()
    pl.semaphore_signal(barrier, inc=1, device_id=(shard, other), device_id_type=MESH)

    @pl.when(has_next)
    def _():
        for r in range(2):
            pl.semaphore_signal(barrier, inc=1, device_id=(shard + 1, r), device_id_type=MESH)

    @pl.when(has_prev)
    def _():
        for r in range(2):
            pl.semaphore_signal(barrier, inc=1, device_id=(shard - 1, r), device_id_type=MESH)

    small_copies = [
        pltpu.make_async_copy(source, target, small_sem.at[k])
        for k, (source, target) in enumerate(
            [
                (counts_hbm, counts),
                (spatial_bias_hbm, spatial_bias),
                (time_bias_hbm, time_bias),
                (gain1_hbm, gain1),
                (bias1_hbm, bias1),
                (gain2_hbm, gain2),
                (bias2_hbm, bias2),
            ]
        )
    ]
    for copy in small_copies:
        copy.start()
    time_copy = pltpu.make_async_copy(time_weight, time_v, in_sem.at[1])
    time_copy.start()

    def start_weight(source, target, sems):
        copies = {}
        for kt in (2, 1, 0):
            for tap in range(9 * kt, 9 * kt + 9):
                copies[tap] = pltpu.make_async_copy(
                    source.at[tap], target.at[:, pl.ds(tap * chans, chans)], sems.at[tap]
                )
                copies[tap].start()
        return copies

    pl.semaphore_wait(
        barrier, 1 + jnp.where(has_next, 2, 0) + jnp.where(has_prev, 2, 0)
    )

    def remote(source, target, index, device, recv=None):
        return pltpu.make_async_remote_copy(
            src_ref=source,
            dst_ref=target,
            send_sem=send_sem.at[index],
            recv_sem=recv_sem.at[index] if recv is None else recv,
            device_id=device,
            device_id_type=MESH,
        )

    halo_copy = remote(video.at[:, 0], halo_v, 0, (shard, other))

    @pl.when(row == 1)
    def _():
        halo_copy.start()
        halo_v[...] = jnp.zeros_like(halo_v)

    padded[...] = jnp.zeros_like(padded)
    hid[0:2] = jnp.zeros((2,) + hid.shape[1:], F32)
    xf[:, :, :, in_cols:] = jnp.zeros(xf.shape[:3] + (xf.shape[3] - in_cols, LANES), F32)

    def spread(line, values):
        values = values.astype(F32)
        for lanes in range(chans // LANES):
            begin = lanes * LANES
            xf[line, lanes, :, 0:in_cols] = values[:, :, begin : begin + LANES]
            for tc in range(3):
                part = xf[line, lanes, :, pl.ds(tc, cols, stride=2), :]
                at = tc * chans + begin
                xs[line, :, at : at + LANES] = part.reshape(slots * cols, LANES).astype(BF16)

    for copy in small_copies:
        copy.wait()
    own_count = counts[shard]
    live = jnp.where(shard == 0, 1, own_count // 2)
    vid_copy.wait()
    for line in range(in_rows):
        spread(line, vid_v[:, line])

    total = None
    for tr in range(3):
        if tr == 2:

            @pl.when(row == 0)
            def _():
                halo_copy.wait_recv()

            spread(in_rows, halo_v[...])
        down_copies[tr].wait()
        lines = jnp.concatenate([xs[2 * r + tr] for r in range(own_rows)], axis=0)
        taps = down_v[3 * tr : 3 * tr + 3].reshape(3 * chans, chans)
        part = jnp.dot(lines, taps, preferred_element_type=F32)
        total = part if total is None else total + part
    reduced = (total + spatial_bias[...].reshape(1, -1)).astype(BF16)
    red_own[...] = reduced
    red_copy = remote(red_own, red_other, 1, (shard, other))
    red_copy.start()

    def to_timeline(values, first_row):
        values = values.astype(F32).reshape(own_rows, slots, cols, chans)
        for f in range(slots):
            timeline[f + 1, pl.ds(first_row, own_rows)] = values[:, f]

    to_timeline(reduced, own_rows * row)
    last_red[...] = (
        timeline[own_count, pl.ds(own_rows * row, own_rows)].reshape(own_rows * cols, chans).astype(BF16)
    )
    before_copies = [
        remote(last_red, before_v.at[row], 2 + r, (shard + 1, r), before_sem.at[row]) for r in range(2)
    ]

    def next_start(copies):
        @pl.when(has_next)
        def _():
            for copy in copies:
                copy.start()

    def prev_wait(copies, buffer):
        @pl.when(has_prev)
        def _():
            for copy in copies:
                copy.wait_recv()

        @pl.when(jnp.logical_not(has_prev))
        def _():
            buffer[...] = jnp.zeros_like(buffer)

    next_start(before_copies)
    w1_copies = start_weight(weight1, w1_v, w1_sem)
    before_waits = [
        remote(last_red, before_v.at[r], 2, (shard, other), before_sem.at[r]) for r in range(2)
    ]

    red_copy.wait_recv()
    to_timeline(red_other[...], own_rows * other)
    time_copy.wait()

    def tap_frames(kt):
        frames = [timeline[2 * t + kt].reshape(plane, chans) for t in range(out_slots)]
        return jnp.concatenate(frames, axis=0).astype(BF16)

    merged = None
    for kt in (2, 1, 0):
        if kt == 0:
            prev_wait(before_waits, before_v)
            timeline[0] = before_v[...].astype(F32).reshape(all_rows, cols, chans)
        part = jnp.dot(tap_frames(kt), time_v[kt], preferred_element_type=F32)
        merged = part if merged is None else merged + part
    merged = merged + time_bias[...].reshape(1, -1)
    first = jnp.where(shard == 0, timeline[1].reshape(plane, chans), merged[:plane])
    latent = round16(jnp.concatenate([first, merged[plane:]], axis=0))
    lat_v[...] = latent.reshape(lat_v.shape)

    def place(first_frame, frames, values):
        padded[first_frame : first_frame + frames, 1 : 1 + all_rows, LEFT : LEFT + cols, :] = values.reshape(
            frames, all_rows, cols, chans
        )
        for kj in range(3):
            begin = LEFT - 1 + kj
            window = padded[first_frame : first_frame + frames, :, begin : begin + cols, :]
            for ki in range(3):
                tap = 3 * ki + kj
                patches[first_frame : first_frame + frames, :, tap * chans : (tap + 1) * chans] = (
                    window[:, ki : ki + all_rows].reshape(frames, plane, chans).astype(BF16)
                )

    def conv_part(kt, target, copies):
        for tap in range(9 * kt, 9 * kt + 9):
            copies[tap].wait()
        lines = patches[kt : kt + out_slots].reshape(out_slots * plane, 9 * chans)
        return dot_t(lines, target[:, 9 * kt * chans : 9 * (kt + 1) * chans])

    act_one = round16(rms_silu(latent, gain1[...].reshape(1, -1)))
    place(2, out_slots, act_one)
    recent = padded[pl.ds(live, 2), 1 : 1 + all_rows, LEFT : LEFT + cols, :]
    last_act[...] = recent.reshape(2 * plane, chans).astype(BF16)
    act_copy = remote(last_act, prior_act, 4, (shard + 1, row))
    next_start([act_copy])
    w2_copies = start_weight(weight2, w2_v, w2_sem)
    acc = conv_part(2, w1_v, w1_copies)
    prev_wait([act_copy], prior_act)
    place(0, 2, prior_act[...].astype(F32))
    for kt in (1, 0):
        acc = acc + conv_part(kt, w1_v, w1_copies)
    part_one = (acc + bias1[...].reshape(1, -1)).astype(BF16)
    h_own[...] = part_one
    h_copy = remote(h_own, h_other, 5, (shard, other))
    h_copy.start()
    hid[2 : 2 + out_slots] = part_one.astype(F32).reshape(out_slots, plane, half)
    h_last[...] = hid[pl.ds(live, 2)].reshape(2 * plane, half).astype(BF16)
    prior_copies = [
        remote(h_last, h_prior.at[row], 6 + r, (shard + 1, r), prior_sem.at[row]) for r in range(2)
    ]
    next_start(prior_copies)
    prior_waits = [
        remote(h_last, h_prior.at[r], 6, (shard, other), prior_sem.at[r]) for r in range(2)
    ]

    h_copy.wait_recv()
    hidden = join(row, part_one.astype(F32), h_other[...].astype(F32))
    place(2, out_slots, rms_silu(hidden, gain2[...].reshape(1, -1)))
    acc = conv_part(2, w2_v, w2_copies)
    prev_wait(prior_waits, h_prior)
    hidden = jnp.concatenate([h_prior[0].astype(F32), h_prior[1].astype(F32)], axis=-1)
    place(0, 2, rms_silu(hidden, gain2[...].reshape(1, -1)))
    for kt in (1, 0):
        acc = acc + conv_part(kt, w2_v, w2_copies)
    part_two = round16(acc + bias2[...].reshape(1, -1)).reshape(out_slots, plane, half)
    hid[2 : 2 + out_slots] = part_two
    rows_of = own_rows * cols

    def share(which):
        return hid[2 : 2 + out_slots, pl.ds(which * rows_of, rows_of)].reshape(out_slots * rows_of, half)

    h2_send[...] = share(other).astype(BF16)
    h2_copy = remote(h2_send, h2_recv, 8, (shard, other))
    h2_copy.start()
    mine = share(row)
    kept = lat_v[:, pl.ds(own_rows * row, own_rows)]

    @pl.when(has_next)
    def _():
        for copy in before_copies + [act_copy] + prior_copies:
            copy.wait_send()

    @pl.when(row == 1)
    def _():
        halo_copy.wait_send()

    red_copy.wait_send()
    h_copy.wait_send()
    h2_copy.wait_recv()
    hidden = join(row, mine, h2_recv[...].astype(F32)).reshape(out_slots, own_rows, cols, chans)
    slot = lax.broadcasted_iota(jnp.int32, hidden.shape, 0)
    out[...] = jnp.where(slot < live, kept + hidden, 0.0).astype(out.dtype)
    h2_copy.wait_send()


def per_device(shards, video, counts, down, sbias, time, tbias, gain1, w1, b1, gain2, w2, b2):
    slots, in_rows, in_cols, chans = video.shape
    out_slots, own_rows, cols = slots // 2, in_rows // 2, in_cols // 2
    all_rows = 2 * own_rows
    half = w1.shape[1]
    plane = all_rows * cols
    hbm = pl.BlockSpec(memory_space=pltpu.HBM)
    dma = pltpu.SemaphoreType.DMA
    return pl.pallas_call(
        functools.partial(kernel, shards),
        out_shape=jax.ShapeDtypeStruct((out_slots, own_rows, cols, chans), BF16),
        in_specs=[hbm] * 12,
        out_specs=pl.BlockSpec(memory_space=pltpu.VMEM),
        scratch_shapes=[
            pltpu.VMEM(video.shape, BF16),
            pltpu.VMEM((slots, in_cols, chans), BF16),
            pltpu.VMEM(down.shape, BF16),
            pltpu.VMEM(time.shape, BF16),
            pltpu.VMEM((half, 27 * chans), BF16),
            pltpu.VMEM((half, 27 * chans), BF16),
            pltpu.VMEM((in_rows + 1, chans // LANES, slots, in_cols + 8, LANES), F32),
            pltpu.VMEM((in_rows + 1, slots * cols, 3 * chans), BF16),
            pltpu.VMEM((slots + 1, all_rows, cols, chans), F32),
            pltpu.VMEM((own_rows * slots * cols, chans), BF16),
            pltpu.VMEM((own_rows * slots * cols, chans), BF16),
            pltpu.VMEM((own_rows * cols, chans), BF16),
            pltpu.VMEM((2, own_rows * cols, chans), BF16),
            pltpu.VMEM((out_slots, all_rows, cols, chans), F32),
            pltpu.VMEM((2 + out_slots, all_rows + 2, cols + 16, chans), F32),
            pltpu.VMEM((2 + out_slots, plane, 9 * chans), BF16),
            pltpu.VMEM((2 * plane, chans), BF16),
            pltpu.VMEM((2 * plane, chans), BF16),
            pltpu.VMEM((2 + out_slots, plane, half), F32),
            pltpu.VMEM((out_slots * plane, half), BF16),
            pltpu.VMEM((out_slots * plane, half), BF16),
            pltpu.VMEM((2 * plane, half), BF16),
            pltpu.VMEM((2, 2 * plane, half), BF16),
            pltpu.VMEM((out_slots * own_rows * cols, half), BF16),
            pltpu.VMEM((out_slots * own_rows * cols, half), BF16),
            dma((2,)),
            dma((3,)),
            dma((27,)),
            dma((27,)),
            dma((9,)),
            dma((9,)),
            dma((2,)),
            dma((2,)),
            pltpu.SMEM(counts.shape, counts.dtype),
            pltpu.VMEM(sbias.shape, F32),
            pltpu.VMEM(tbias.shape, F32),
            pltpu.VMEM(gain1.shape, F32),
            pltpu.VMEM(b1.shape, F32),
            pltpu.VMEM(gain2.shape, F32),
            pltpu.VMEM(b2.shape, F32),
            dma((7,)),
        ],
        compiler_params=pltpu.CompilerParams(
            collective_id=0, has_side_effects=True, vmem_limit_bytes=62 * 1024 * 1024
        ),
        name="section",
    )(video, counts, down, sbias, time, tbias, gain1, w1, b1, gain2, w2, b2)


def solution(mesh):
    in_specs = (
        P("frames", "rows", None, None),
        P(),
        P(),
        P(),
        P(),
        P(),
        P(),
        P(None, "rows", None),
        P("rows"),
        P(),
        P(None, "rows", None),
        P("rows"),
    )
    return jax.shard_map(
        functools.partial(per_device, mesh.shape["frames"]),
        mesh=mesh,
        in_specs=in_specs,
        out_specs=P("frames", "rows", None, None),
        check_vma=False,
    )
```

```python
import functools

import jax
import jax.numpy as jnp
from jax import lax
from jax.experimental import pallas as pl
from jax.experimental.pallas import tpu as pltpu
from jax.sharding import PartitionSpec as P

MESH = pl.DeviceIdType.MESH
F32 = jnp.float32
BF16 = jnp.bfloat16
EPSILON = 1e-06
LANES = 128
LEFT = 8


def rms_silu(values, gain):
    mean_sq = jnp.mean(values * values, axis=-1, keepdims=True)
    return jax.nn.silu(values * lax.rsqrt(mean_sq + EPSILON) * gain)


def round16(values):
    return values.astype(BF16).astype(F32)


def join(row, own, other):
    low = jnp.where(row == 0, own, other)
    high = jnp.where(row == 0, other, own)
    return jnp.concatenate([low, high], axis=-1)


def dot_t(values, weight):
    turned = lax.dot_general(weight, values, (((1,), (1,)), ((), ())), preferred_element_type=F32)
    return turned.T


def kernel(
    shards,
    video,
    counts_hbm,
    down_weight,
    spatial_bias_hbm,
    time_weight,
    time_bias_hbm,
    gain1_hbm,
    weight1,
    bias1_hbm,
    gain2_hbm,
    weight2,
    bias2_hbm,
    out,
    vid_v,
    halo_v,
    down_v,
    time_v,
    w1_v,
    w2_v,
    xf,
    xs,
    timeline,
    red_own,
    red_other,
    last_red,
    before_v,
    lat_v,
    padded,
    patches,
    last_act,
    prior_act,
    hid,
    h_own,
    h_other,
    h_last,
    h_prior,
    h2_send,
    h2_recv,
    in_sem,
    down_sem,
    w1_sem,
    w2_sem,
    send_sem,
    recv_sem,
    before_sem,
    prior_sem,
    counts,
    spatial_bias,
    time_bias,
    gain1,
    bias1,
    gain2,
    bias2,
    small_sem,
):
    shard = lax.axis_index("frames")
    row = lax.axis_index("rows")
    other = 1 - row
    slots, in_rows, in_cols, chans = vid_v.shape
    out_slots, own_rows, cols = slots // 2, in_rows // 2, in_cols // 2
    all_rows = 2 * own_rows
    half = h_own.shape[1]
    plane = all_rows * cols
    has_next = shard < shards - 1
    has_prev = shard > 0

    vid_copy = pltpu.make_async_copy(video, vid_v, in_sem.at[0])
    vid_copy.start()
    down_copies = []
    for k in range(3):
        copy = pltpu.make_async_copy(
            down_weight.at[pl.ds(3 * k, 3)], down_v.at[pl.ds(3 * k, 3)], down_sem.at[k]
        )
        copy.start()
        down_copies.append(copy)

    barrier = pltpu.get_barrier_semaphore()
    pl.semaphore_signal(barrier, inc=1, device_id=(shard, other), device_id_type=MESH)

    @pl.when(has_next)
    def _():
        for r in range(2):
            pl.semaphore_signal(barrier, inc=1, device_id=(shard + 1, r), device_id_type=MESH)

    @pl.when(has_prev)
    def _():
        for r in range(2):
            pl.semaphore_signal(barrier, inc=1, device_id=(shard - 1, r), device_id_type=MESH)

    small_copies = [
        pltpu.make_async_copy(source, target, small_sem.at[k])
        for k, (source, target) in enumerate(
            [
                (counts_hbm, counts),
                (spatial_bias_hbm, spatial_bias),
                (time_bias_hbm, time_bias),
                (gain1_hbm, gain1),
                (bias1_hbm, bias1),
                (gain2_hbm, gain2),
                (bias2_hbm, bias2),
            ]
        )
    ]
    for copy in small_copies:
        copy.start()
    time_copy = pltpu.make_async_copy(time_weight, time_v, in_sem.at[1])
    time_copy.start()

    def start_weight(source, target, sems):
        copies = {}
        for kt in (2, 1, 0):
            for tap in range(9 * kt, 9 * kt + 9):
                copies[tap] = pltpu.make_async_copy(
                    source.at[tap], target.at[:, pl.ds(tap * chans, chans)], sems.at[tap]
                )
                copies[tap].start()
        return copies

    pl.semaphore_wait(
        barrier, 1 + jnp.where(has_next, 2, 0) + jnp.where(has_prev, 2, 0)
    )

    def remote(source, target, index, device, recv=None):
        return pltpu.make_async_remote_copy(
            src_ref=source,
            dst_ref=target,
            send_sem=send_sem.at[index],
            recv_sem=recv_sem.at[index] if recv is None else recv,
            device_id=device,
            device_id_type=MESH,
        )

    halo_copy = remote(video.at[:, 0], halo_v, 0, (shard, other))

    @pl.when(row == 1)
    def _():
        halo_copy.start()
        halo_v[...] = jnp.zeros_like(halo_v)

    padded[...] = jnp.zeros_like(padded)
    hid[0:2] = jnp.zeros((2,) + hid.shape[1:], F32)
    xf[:, :, :, in_cols:] = jnp.zeros(xf.shape[:3] + (xf.shape[3] - in_cols, LANES), F32)

    def spread(line, values):
        values = values.astype(F32)
        for lanes in range(chans // LANES):
            begin = lanes * LANES
            xf[line, lanes, :, 0:in_cols] = values[:, :, begin : begin + LANES]
            for tc in range(3):
                part = xf[line, lanes, :, pl.ds(tc, cols, stride=2), :]
                at = tc * chans + begin
                xs[line, :, at : at + LANES] = part.reshape(slots * cols, LANES).astype(BF16)

    for copy in small_copies:
        copy.wait()
    own_count = counts[shard]
    live = jnp.where(shard == 0, 1, own_count // 2)
    vid_copy.wait()
    for line in range(in_rows):
        spread(line, vid_v[:, line])

    total = None
    for tr in range(3):
        if tr == 2:

            @pl.when(row == 0)
            def _():
                halo_copy.wait_recv()

            spread(in_rows, halo_v[...])
        down_copies[tr].wait()
        lines = jnp.concatenate([xs[2 * r + tr] for r in range(own_rows)], axis=0)
        taps = down_v[3 * tr : 3 * tr + 3].reshape(3 * chans, chans)
        part = jnp.dot(lines, taps, preferred_element_type=F32)
        total = part if total is None else total + part
    reduced = (total + spatial_bias[...].reshape(1, -1)).astype(BF16)
    red_own[...] = reduced
    red_copy = remote(red_own, red_other, 1, (shard, other))
    red_copy.start()

    def to_timeline(values, first_row):
        values = values.astype(F32).reshape(own_rows, slots, cols, chans)
        for f in range(slots):
            timeline[f + 1, pl.ds(first_row, own_rows)] = values[:, f]

    to_timeline(reduced, own_rows * row)
    last_red[...] = (
        timeline[own_count, pl.ds(own_rows * row, own_rows)].reshape(own_rows * cols, chans).astype(BF16)
    )
    before_copies = [
        remote(last_red, before_v.at[row], 2 + r, (shard + 1, r), before_sem.at[row]) for r in range(2)
    ]

    def next_start(copies):
        @pl.when(has_next)
        def _():
            for copy in copies:
                copy.start()

    def prev_wait(copies, buffer):
        @pl.when(has_prev)
        def _():
            for copy in copies:
                copy.wait_recv()

        @pl.when(jnp.logical_not(has_prev))
        def _():
            buffer[...] = jnp.zeros_like(buffer)

    next_start(before_copies)
    w1_copies = start_weight(weight1, w1_v, w1_sem)
    before_waits = [
        remote(last_red, before_v.at[r], 2, (shard, other), before_sem.at[r]) for r in range(2)
    ]

    red_copy.wait_recv()
    to_timeline(red_other[...], own_rows * other)
    time_copy.wait()

    def place(first_frame, frames, values):
        padded[first_frame : first_frame + frames, 1 : 1 + all_rows, LEFT : LEFT + cols, :] = values.reshape(
            frames, all_rows, cols, chans
        )
        for kj in range(3):
            begin = LEFT - 1 + kj
            window = padded[first_frame : first_frame + frames, :, begin : begin + cols, :]
            for ki in range(3):
                tap = 3 * ki + kj
                patches[first_frame : first_frame + frames, :, tap * chans : (tap + 1) * chans] = (
                    window[:, ki : ki + all_rows].reshape(frames, plane, chans).astype(BF16)
                )

    def conv(target, copies, prior):
        def part(kt, first_slot, end_slot):
            frames = end_slot - first_slot
            lines = patches[kt + first_slot : kt + end_slot].reshape(frames * plane, 9 * chans)
            return dot_t(lines, target[:, 9 * kt * chans : 9 * (kt + 1) * chans])

        def arrive(kt):
            for tap in range(9 * kt, 9 * kt + 9):
                copies[tap].wait()

        arrive(2)
        total = part(2, 0, out_slots)
        arrive(1)
        one = part(1, 1, out_slots)
        arrive(0)
        two = part(0, 2, out_slots)
        prior()
        one = jnp.concatenate([part(1, 0, 1), one], axis=0)
        two = jnp.concatenate([part(0, 0, 2), two], axis=0)
        return total + one + two

    def time_part(kt, first_slot, end_slot):
        frames = [timeline[2 * t + kt].reshape(plane, chans) for t in range(first_slot, end_slot)]
        lines = jnp.concatenate(frames, axis=0).astype(BF16)
        return jnp.dot(lines, time_v[kt], preferred_element_type=F32)

    base = time_part(2, 0, out_slots) + time_part(1, 0, out_slots) + time_bias[...].reshape(1, -1)
    later = round16(base[plane:] + time_part(0, 1, out_slots))
    lat_v[1:] = later.reshape((out_slots - 1,) + lat_v.shape[1:])
    place(3, out_slots - 1, round16(rms_silu(later, gain1[...].reshape(1, -1))))
    whole = timeline[1].reshape(plane, chans)
    padded[2, 1 : 1 + all_rows, LEFT : LEFT + cols, :] = round16(
        rms_silu(whole, gain1[...].reshape(1, -1))
    ).reshape(all_rows, cols, chans)
    act_copies = [remote(last_act.at[k], prior_act.at[k], 4 + 5 * k, (shard + 1, row)) for k in range(2)]

    def recent(k):
        frame = padded[live + k, 1 : 1 + all_rows, LEFT : LEFT + cols, :]
        last_act[k] = frame.reshape(plane, chans).astype(BF16)
        next_start([act_copies[k]])

    recent(1)
    prev_wait(before_waits, before_v)
    timeline[0] = before_v[...].astype(F32).reshape(all_rows, cols, chans)
    first = round16(jnp.where(shard == 0, whole, base[:plane] + time_part(0, 0, 1)))
    lat_v[0] = first.reshape(all_rows, cols, chans)
    place(2, 1, round16(rms_silu(first, gain1[...].reshape(1, -1))))
    recent(0)
    w2_copies = start_weight(weight2, w2_v, w2_sem)

    def prior_one():
        prev_wait(act_copies, prior_act)
        place(0, 2, prior_act[...].astype(F32))

    acc = conv(w1_v, w1_copies, prior_one)
    part_one = (acc + bias1[...].reshape(1, -1)).astype(BF16)
    h_own[...] = part_one
    h_copy = remote(h_own, h_other, 5, (shard, other))
    h_copy.start()
    hid[2 : 2 + out_slots] = part_one.astype(F32).reshape(out_slots, plane, half)
    h_last[...] = hid[pl.ds(live, 2)].reshape(2 * plane, half).astype(BF16)
    prior_copies = [
        remote(h_last, h_prior.at[row], 6 + r, (shard + 1, r), prior_sem.at[row]) for r in range(2)
    ]
    next_start(prior_copies)
    prior_waits = [
        remote(h_last, h_prior.at[r], 6, (shard, other), prior_sem.at[r]) for r in range(2)
    ]

    h_copy.wait_recv()
    hidden = join(row, part_one.astype(F32), h_other[...].astype(F32))
    place(2, out_slots, rms_silu(hidden, gain2[...].reshape(1, -1)))

    def prior_two():
        prev_wait(prior_waits, h_prior)
        hidden = jnp.concatenate([h_prior[0].astype(F32), h_prior[1].astype(F32)], axis=-1)
        place(0, 2, rms_silu(hidden, gain2[...].reshape(1, -1)))

    acc = conv(w2_v, w2_copies, prior_two)
    part_two = round16(acc + bias2[...].reshape(1, -1)).reshape(out_slots, plane, half)
    hid[2 : 2 + out_slots] = part_two
    rows_of = own_rows * cols

    def share(which):
        return hid[2 : 2 + out_slots, pl.ds(which * rows_of, rows_of)].reshape(out_slots * rows_of, half)

    h2_send[...] = share(other).astype(BF16)
    h2_copy = remote(h2_send, h2_recv, 8, (shard, other))
    h2_copy.start()
    mine = share(row)
    kept = lat_v[:, pl.ds(own_rows * row, own_rows)]

    @pl.when(has_next)
    def _():
        for copy in before_copies + act_copies + prior_copies:
            copy.wait_send()

    @pl.when(row == 1)
    def _():
        halo_copy.wait_send()

    red_copy.wait_send()
    h_copy.wait_send()
    h2_copy.wait_recv()
    hidden = join(row, mine, h2_recv[...].astype(F32)).reshape(out_slots, own_rows, cols, chans)
    slot = lax.broadcasted_iota(jnp.int32, hidden.shape, 0)
    out[...] = jnp.where(slot < live, kept + hidden, 0.0).astype(out.dtype)
    h2_copy.wait_send()


def per_device(shards, video, counts, down, sbias, time, tbias, gain1, w1, b1, gain2, w2, b2):
    slots, in_rows, in_cols, chans = video.shape
    out_slots, own_rows, cols = slots // 2, in_rows // 2, in_cols // 2
    all_rows = 2 * own_rows
    half = w1.shape[1]
    plane = all_rows * cols
    hbm = pl.BlockSpec(memory_space=pltpu.HBM)
    dma = pltpu.SemaphoreType.DMA
    return pl.pallas_call(
        functools.partial(kernel, shards),
        out_shape=jax.ShapeDtypeStruct((out_slots, own_rows, cols, chans), BF16),
        in_specs=[hbm] * 12,
        out_specs=pl.BlockSpec(memory_space=pltpu.VMEM),
        scratch_shapes=[
            pltpu.VMEM(video.shape, BF16),
            pltpu.VMEM((slots, in_cols, chans), BF16),
            pltpu.VMEM(down.shape, BF16),
            pltpu.VMEM(time.shape, BF16),
            pltpu.VMEM((half, 27 * chans), BF16),
            pltpu.VMEM((half, 27 * chans), BF16),
            pltpu.VMEM((in_rows + 1, chans // LANES, slots, in_cols + 8, LANES), F32),
            pltpu.VMEM((in_rows + 1, slots * cols, 3 * chans), BF16),
            pltpu.VMEM((slots + 1, all_rows, cols, chans), F32),
            pltpu.VMEM((own_rows * slots * cols, chans), BF16),
            pltpu.VMEM((own_rows * slots * cols, chans), BF16),
            pltpu.VMEM((own_rows * cols, chans), BF16),
            pltpu.VMEM((2, own_rows * cols, chans), BF16),
            pltpu.VMEM((out_slots, all_rows, cols, chans), F32),
            pltpu.VMEM((2 + out_slots, all_rows + 2, cols + 16, chans), F32),
            pltpu.VMEM((2 + out_slots, plane, 9 * chans), BF16),
            pltpu.VMEM((2, plane, chans), BF16),
            pltpu.VMEM((2, plane, chans), BF16),
            pltpu.VMEM((2 + out_slots, plane, half), F32),
            pltpu.VMEM((out_slots * plane, half), BF16),
            pltpu.VMEM((out_slots * plane, half), BF16),
            pltpu.VMEM((2 * plane, half), BF16),
            pltpu.VMEM((2, 2 * plane, half), BF16),
            pltpu.VMEM((out_slots * own_rows * cols, half), BF16),
            pltpu.VMEM((out_slots * own_rows * cols, half), BF16),
            dma((2,)),
            dma((3,)),
            dma((27,)),
            dma((27,)),
            dma((10,)),
            dma((10,)),
            dma((2,)),
            dma((2,)),
            pltpu.SMEM(counts.shape, counts.dtype),
            pltpu.VMEM(sbias.shape, F32),
            pltpu.VMEM(tbias.shape, F32),
            pltpu.VMEM(gain1.shape, F32),
            pltpu.VMEM(b1.shape, F32),
            pltpu.VMEM(gain2.shape, F32),
            pltpu.VMEM(b2.shape, F32),
            dma((7,)),
        ],
        compiler_params=pltpu.CompilerParams(
            collective_id=0, has_side_effects=True, vmem_limit_bytes=62 * 1024 * 1024
        ),
        name="section",
    )(video, counts, down, sbias, time, tbias, gain1, w1, b1, gain2, w2, b2)


def solution(mesh):
    in_specs = (
        P("frames", "rows", None, None),
        P(),
        P(),
        P(),
        P(),
        P(),
        P(),
        P(None, "rows", None),
        P("rows"),
        P(),
        P(None, "rows", None),
        P("rows"),
    )
    return jax.shard_map(
        functools.partial(per_device, mesh.shape["frames"]),
        mesh=mesh,
        in_specs=in_specs,
        out_specs=P("frames", "rows", None, None),
        check_vma=False,
    )
```
